32 devices in a mesh: row: 8 (over z, y), col: 4 (over x, core).
Axes of the slice: x: 2, y: 2, z: 4, core: 2. Of those that a mesh axis runs over, the one named last changes fastest.
Arguments:
- attn_in: bfloat16 [256, 16384], P('row', 'col'), may hold values from -6 to 6
- w_out: bfloat16 [16384, 16384], P('col', 'row'), may hold values from -0.046875 to 0.046875
- resid: bfloat16 [256, 16384], P('col', 'row'), may hold values from -64 to 64, as said below
- norm_gain: float32 [16384], P('row'), may hold values from 0.1 to 1.9
- w_gate: bfloat16 [16384, 26624], P('row', 'col'), may hold values from -0.046875 to 0.046875
- w_up: bfloat16 [16384, 26624], P('row', 'col'), may hold values from -0.046875 to 0.046875
- w_down: bfloat16 [26624, 16384], P('col', 'row'), may hold values from -0.0390625 to 0.0390625
Outputs:
- layer_out: bfloat16 [256, 16384], P('col', 'row')
The draws below stay inside these ranges and needn't reach their ends.
Inputs may be any that keep to these rules, and one draw needn't show every extreme that they name: `resid`: entries are real-valued and not all of one size.
All inputs are finite; a program needn't handle non-finite values.
Results may differ from the reference program's by a relative error of at most 0.0051.
Values may be sent and summed in bfloat16 or wider, within the bound.
A program may use at most 192 MiB of HBM per device.

```python
import jax
import jax.numpy as jnp
from jax import lax

D = 16384
FF = 26624
TOKENS = 256


def draw_resid(key, part):
    k_base = jax.random.fold_in(key, 11)
    k_rows = jax.random.fold_in(key, 12)
    k_cols = jax.random.fold_in(key, 13)
    column = jnp.arange(D, dtype=jnp.float32) / D
    ramp = jnp.exp(0.5 * jnp.log(3.0) * column)
    col_scale = jnp.exp(jax.random.uniform(k_cols, (D,), jnp.float32, jnp.log(0.5), jnp.log(3.0))) * ramp
    row_scale = jnp.exp(jax.random.uniform(k_rows, (TOKENS, 1), jnp.float32, jnp.log(0.3), jnp.log(3.0)))
    base = jnp.clip(jax.random.normal(k_base, (TOKENS, D), jnp.float32), -4.0, 4.0)
    values = base * row_scale * col_scale[None, :]
    return jnp.clip(values, -64.0, 64.0).astype(jnp.bfloat16)


def steps_of(own_key, shape, split, smallest, largest):
    loudness, own = 1.0, jax.random.fold_in(own_key, 6)
    for position, blocks in split:
        draws = jnp.exp(jax.random.uniform(jax.random.fold_in(own, position), (blocks,), jnp.float32, smallest / len(split), largest / len(split)))
        loudness = loudness * jnp.repeat(draws, shape[position] // blocks).reshape([-1 if axis == position else 1 for axis in range(len(shape))])
    return loudness


def centred(key, dims, spread, limit, split=(), kind=jnp.bfloat16):
    entries = jax.random.normal(key, dims, jnp.float32) * spread
    if len(split) > 0:
        entries = steps_of(key, dims, split, -0.22, 0.18) * entries
    return jnp.clip(entries, min=-limit, max=limit).astype(kind)


def setup_inputs(seed: int = 0) -> dict:
    keys = jax.random.split(jax.random.key(seed), 8)
    return {
        "attn_in": centred(keys[0], (TOKENS, D), 1.0, 6.0, ((0, 8), (1, 4))),
        "w_out": centred(keys[1], (D, D), D ** -0.5, 0.046875, ((0, 4), (1, 8))),
        "resid": draw_resid(jax.random.fold_in(keys[7], 71), 0),
        "norm_gain": jnp.clip(1.0 + 0.18 * jax.random.normal(keys[3], (D,), jnp.float32), 0.1, 1.9),
        "w_gate": centred(keys[4], (D, FF), D ** -0.5, 0.046875, ((0, 8), (1, 4))),
        "w_up": centred(keys[5], (D, FF), D ** -0.5, 0.046875, ((0, 8), (1, 4))),
        "w_down": centred(keys[6], (FF, D), FF ** -0.5, 0.0390625, ((0, 4), (1, 8))),
    }


def reference(attn_in, w_out, resid, norm_gain, w_gate, w_up, w_down):
    projected = jnp.dot(attn_in, w_out, preferred_element_type=jnp.float32)
    stream = (resid.astype(jnp.float32) + projected).astype(jnp.bfloat16)
    stream_f = stream.astype(jnp.float32)
    mean_square = lax.optimization_barrier(jnp.mean(stream_f * stream_f, axis=1, keepdims=True))
    normed = (stream_f * lax.rsqrt(mean_square + 1e-05) * norm_gain[None, :]).astype(jnp.bfloat16)
    gate = jnp.dot(normed, w_gate, preferred_element_type=jnp.float32)
    up_part = jnp.dot(normed, w_up, preferred_element_type=jnp.float32)
    activated = (jax.nn.silu(gate) * up_part).astype(jnp.bfloat16)
    down = jnp.dot(activated, w_down, preferred_element_type=jnp.float32)
    return (stream_f + down).astype(jnp.bfloat16)
```

```python
import functools

import jax
import jax.numpy as jnp
from jax import lax
from jax.experimental import pallas as pl
from jax.experimental.pallas import tpu as pltpu
from jax.sharding import PartitionSpec as P

MESH = pl.DeviceIdType.MESH
F32, BF16 = jnp.float32, jnp.bfloat16
epsilon = 1e-05
SLOTS = 3


def chunk_of(hidden):
    return max(c for c in range(128, 513, 128) if hidden % c == 0)


def grid_of(rows):
    inner = 1
    while (2 * inner) ** 2 <= rows:
        inner *= 2
    return rows // inner, inner


def layer_kernel(
    Z, Y, Q, T, C, NF, NC,
    attn, w_out, resid, gain, w_gate, w_up, w_down,
    out,
    wo_buf, wg_buf, wu_buf,
    feat, ysend, yrecv, zrecv, act,
    acc, normed, stream, dsend, drecv1, drecv2, sq_send, sq_recv,
    wo_sem, wg_sem, wu_sem, wd_sem,
    f_zs, f_zr, f_ys, f_yr,
    r_ys, r_yr, r_zs, r_zr,
    a_zs, a_zr, a_ys, a_yr,
    p_s, p_r, d_s, d_r, q_s, q_r, n_s, n_r,
):
    n = Z * Y
    row, col = lax.axis_index("row"), lax.axis_index("col")
    z, y = row // Y, lax.rem(row, Y)
    tokens, width = normed.shape
    TB = tokens // Q

    def z_peer(d):
        return lax.rem(z + d, Z)

    def y_peer(d):
        return lax.rem(y + d, Y)

    def to_row(src, dst, send, recv, peer):
        return pltpu.make_async_remote_copy(
            src_ref=src, dst_ref=dst, send_sem=send, recv_sem=recv,
            device_id={"row": peer}, device_id_type=MESH,
        )

    def to_col(src, dst, send, recv, peer):
        return pltpu.make_async_remote_copy(
            src_ref=src, dst_ref=dst, send_sem=send, recv_sem=recv,
            device_id={"col": peer}, device_id_type=MESH,
        )

    def columns(c):
        return pl.ds(pl.multiple_of(c * C, C), C)

    def load_wo(f):
        return pltpu.make_async_copy(w_out.at[columns(f)], wo_buf.at[f], wo_sem.at[f])

    def load_gu(c):
        s = lax.rem(c, SLOTS)
        return (
            pltpu.make_async_copy(w_gate.at[:, columns(c)], wg_buf.at[s], wg_sem.at[s]),
            pltpu.make_async_copy(w_up.at[:, columns(c)], wu_buf.at[s], wu_sem.at[s]),
        )

    def load_wd(c):
        s = lax.rem(c, NF)
        return pltpu.make_async_copy(w_down.at[columns(c)], wo_buf.at[s], wd_sem.at[s])

    @pl.loop(0, NF)
    def _(f):
        load_wo(f).start()

    @pl.loop(0, SLOTS)
    def _(c):
        for copy in load_gu(c):
            copy.start()

    barrier = pltpu.get_barrier_semaphore()
    for d in range(1, n):
        pl.semaphore_signal(barrier, inc=1, device_id={"row": lax.rem(row + d, n)}, device_id_type=MESH)
    for d in range(1, Q):
        pl.semaphore_signal(barrier, inc=1, device_id={"col": lax.rem(col + d, Q)}, device_id_type=MESH)
    pl.semaphore_wait(barrier, n - 1 + Q - 1)

    def gather_z(buf, c, zs, zr):
        return [
            to_row(buf.at[c, y, z], buf.at[c, y, z], zs.at[c, d - 1], zr.at[c, d - 1], z_peer(d) * Y + y)
            for d in range(1, Z)
        ]

    def gather_y(buf, c, ys, yr):
        return [
            to_row(buf.at[c, y], buf.at[c, y], ys.at[c, d - 1], yr.at[c, d - 1], z * Y + y_peer(d))
            for d in range(1, Y)
        ]

    def reduce_cols(recv, s_sem, r_sem):
        for r in range(n):
            at = ((r % Y) * Z + r // Y) * T
            dsend[r * T : (r + 1) * T] = acc[at : at + T].astype(BF16)
        copies = []
        for d in range(1, Q):
            peer = lax.rem(col + d, Q)
            copies.append(
                to_col(
                    dsend.at[pl.ds(pl.multiple_of(peer * TB, TB), TB)],
                    recv.at[d - 1], s_sem.at[d - 1], r_sem.at[d - 1], peer,
                )
            )
        for copy in copies:
            copy.start()
        total = dsend[pl.ds(pl.multiple_of(col * TB, TB), TB)].astype(F32)
        for copy in copies:
            copy.wait()
        for d in range(Q - 1):
            total = total + recv[d].astype(F32)
        return total

    for f in range(NF):
        feat[f, y, z] = attn[:, f * C : (f + 1) * C]
    acc[...] = jnp.zeros_like(acc)

    @pl.loop(0, NF)
    def _(f):
        for copy in gather_z(feat, f, f_zs, f_zr):
            copy.start()

    @pl.loop(0, NF + 1)
    def _(t):
        @pl.when(t < NF)
        def _():
            for copy in gather_z(feat, t, f_zs, f_zr):
                copy.wait_recv()
            for copy in gather_y(feat, t, f_ys, f_yr):
                copy.start()

        @pl.when(t >= 1)
        def _():
            f = t - 1
            for copy in gather_y(feat, f, f_ys, f_yr):
                copy.wait()
            for copy in gather_z(feat, f, f_zs, f_zr):
                copy.wait_send()
            load_wo(f).wait()
            acc[...] += jnp.dot(feat[f].reshape(tokens, C), wo_buf[f], preferred_element_type=F32)

    @pl.loop(0, min(NF, NC))
    def _(c):
        load_wd(c).start()

    stream_now = (resid[...].astype(F32) + reduce_cols(drecv1, p_s, p_r)).astype(BF16)
    stream[...] = stream_now
    stream_f = stream_now.astype(F32)

    sq_send[...] = jnp.broadcast_to(jnp.sum(stream_f * stream_f, axis=1, keepdims=True), sq_send.shape)
    copies = [
        to_row(sq_send, sq_recv.at[d - 1], q_s.at[d - 1], q_r.at[d - 1], lax.rem(row + d, n))
        for d in range(1, n)
    ]
    for copy in copies:
        copy.start()
    acc[...] = jnp.zeros_like(acc)
    for copy in copies:
        copy.wait()
    squares = sq_send[...]
    for d in range(n - 1):
        squares = squares + sq_recv[d]
    scale = lax.rsqrt(squares[:, :1] / (width * n) + epsilon)
    own = pl.ds(pl.multiple_of(col * TB, TB), TB)
    normed[own] = (stream[...].astype(F32) * scale * gain[...]).astype(BF16)
    copies = [
        to_col(normed.at[own], normed.at[own], n_s.at[d - 1], n_r.at[d - 1], lax.rem(col + d, Q))
        for d in range(1, Q)
    ]
    for copy in copies:
        copy.start()
    for copy in copies:
        copy.wait()

    def reduce_y(c):
        return [
            to_row(ysend.at[c, y_peer(d)], yrecv.at[c, d - 1], r_ys.at[c, d - 1], r_yr.at[c, d - 1], z * Y + y_peer(d))
            for d in range(1, Y)
        ]

    def reduce_z(c):
        return [
            to_row(ysend.at[c, y, z_peer(d)], zrecv.at[c, d - 1], r_zs.at[c, d - 1], r_zr.at[c, d - 1], z_peer(d) * Y + y)
            for d in range(1, Z)
        ]

    def multiply(c):
        s = lax.rem(c, SLOTS)
        gate_copy, up_copy = load_gu(c)
        for half, copy, buf in ((0, gate_copy, wg_buf), (1, up_copy, wu_buf)):
            copy.wait()
            part = jnp.dot(normed[...], buf[s], preferred_element_type=F32).astype(BF16)
            for r in range(n):
                ysend[c, r % Y, r // Y, :, half * C : (half + 1) * C] = part[r * T : (r + 1) * T]
        for copy in reduce_y(c):
            copy.start()

        @pl.when(c + SLOTS < NC)
        def _():
            for copy in load_gu(c + SLOTS):
                copy.start()

    def add_y(c):
        for copy in reduce_y(c):
            copy.wait_recv()
        total = ysend[c, y].astype(F32)
        for d in range(Y - 1):
            total = total + yrecv[c, d].astype(F32)
        ysend[c, y] = total.astype(BF16)
        for copy in reduce_z(c):
            copy.start()

    def activate(c):
        for copy in reduce_z(c):
            copy.wait_recv()
        total = ysend[c, y, z].astype(F32)
        for d in range(Z - 1):
            total = total + zrecv[c, d].astype(F32)
        gate, up = total[:, :C], total[:, C:]
        act[c, y, z] = (gate / (1.0 + jnp.exp(-gate)) * up).astype(BF16)
        for copy in gather_z(act, c, a_zs, a_zr):
            copy.start()

    def pass_on(c):
        for copy in gather_z(act, c, a_zs, a_zr):
            copy.wait_recv()
        for copy in gather_y(act, c, a_ys, a_yr):
            copy.start()

    def project_down(c):
        for copy in gather_y(act, c, a_ys, a_yr):
            copy.wait()
        for copy in gather_z(act, c, a_zs, a_zr) + reduce_y(c) + reduce_z(c):
            copy.wait_send()
        load_wd(c).wait()
        acc[...] += jnp.dot(act[c].reshape(tokens, C), wo_buf[lax.rem(c, NF)], preferred_element_type=F32)

        @pl.when(c + NF < NC)
        def _():
            load_wd(c + NF).start()

    stages = ((0, multiply), (2, add_y), (3, activate), (4, pass_on), (5, project_down))

    @pl.loop(0, NC + 5)
    def _(t):
        for lag, stage in stages:

            @pl.when((t >= lag) & (t < NC + lag))
            def _():
                stage(t - lag)

    out[...] = (stream[...].astype(F32) + reduce_cols(drecv2, d_s, d_r)).astype(out.dtype)


def on_device(Z, Y, Q, attn_in, w_out, resid, norm_gain, w_gate, w_up, w_down):
    n = Z * Y
    T, features = attn_in.shape
    width, hidden = w_gate.shape
    tokens = T * n
    TB = tokens // Q
    C = chunk_of(hidden)
    NF, NC = features // C, hidden // C
    dma = pltpu.SemaphoreType.DMA
    vmem, hbm = pl.BlockSpec(memory_space=pltpu.VMEM), pl.BlockSpec(memory_space=pl.ANY)

    def pairs(count, peers):
        return [dma((count, peers)), dma((count, peers))]

    def both(peers):
        return [dma((peers,)), dma((peers,))]

    return pl.pallas_call(
        functools.partial(layer_kernel, Z, Y, Q, T, C, NF, NC),
        out_shape=jax.ShapeDtypeStruct((TB, width), BF16),
        in_specs=[vmem, hbm, vmem, vmem, hbm, hbm, hbm],
        out_specs=vmem,
        scratch_shapes=[
            pltpu.VMEM((NF, C, width), BF16),
            pltpu.VMEM((SLOTS, width, C), BF16),
            pltpu.VMEM((SLOTS, width, C), BF16),
            pltpu.VMEM((NF, Y, Z, T, C), BF16),
            pltpu.VMEM((NC, Y, Z, T, 2 * C), BF16),
            pltpu.VMEM((NC, Y - 1, Z, T, 2 * C), BF16),
            pltpu.VMEM((NC, Z - 1, T, 2 * C), BF16),
            pltpu.VMEM((NC, Y, Z, T, C), BF16),
            pltpu.VMEM((tokens, width), F32),
            pltpu.VMEM((tokens, width), BF16),
            pltpu.VMEM((TB, width), BF16),
            pltpu.VMEM((tokens, width), BF16),
            pltpu.VMEM((Q - 1, TB, width), BF16),
            pltpu.VMEM((Q - 1, TB, width), BF16),
            pltpu.VMEM((TB, 128), F32),
            pltpu.VMEM((n - 1, TB, 128), F32),
            dma((NF,)), dma((SLOTS,)), dma((SLOTS,)), dma((NF,)),
            *pairs(NF, Z - 1), *pairs(NF, Y - 1),
            *pairs(NC, Y - 1), *pairs(NC, Z - 1),
            *pairs(NC, Z - 1), *pairs(NC, Y - 1),
            *both(Q - 1), *both(Q - 1), *both(n - 1), *both(Q - 1),
        ],
        compiler_params=pltpu.CompilerParams(
            collective_id=0, has_side_effects=True, vmem_limit_bytes=60 * 2**20
        ),
    )(attn_in, w_out, resid, norm_gain.reshape(1, width), w_gate, w_up, w_down)


def solution(mesh):
    Z, Y = grid_of(mesh.shape["row"])
    placed = (
        P("row", "col"),
        P("col", "row"),
        P("col", "row"),
        P("row"),
        P("row", "col"),
        P("row", "col"),
        P("col", "row"),
    )
    return jax.shard_map(
        functools.partial(on_device, Z, Y, mesh.shape["col"]),
        mesh=mesh, in_specs=placed, out_specs=P("col", "row"), check_vma=False,
    )
```

```python
import functools

import jax
import jax.numpy as jnp
from jax import lax
from jax.experimental import pallas as pl
from jax.experimental.pallas import tpu as pltpu
from jax.sharding import PartitionSpec as P

MESH = pl.DeviceIdType.MESH
F32, BF16 = jnp.float32, jnp.bfloat16
epsilon = 1e-05
SLOTS = 3
CORES = 2


def chunk_of(hidden):
    return max(c for c in range(128, 513, 128) if hidden % c == 0)


def grid_of(rows):
    inner = 1
    while (2 * inner) ** 2 <= rows:
        inner *= 2
    return rows // inner, inner


def layer_kernel(
    Z, Y, Q, T, C, NF, NC,
    attn, w_out, resid, gain, w_gate, w_up, w_down,
    out,
    wo_buf, wg_buf, wu_buf,
    feat, ysend, yrecv, zrecv, act,
    acc, normed, stream, dsend, core_recv1, x_recv1, core_recv2, x_recv2, squares, sq_recv, scale,
    wo_sem, wg_sem, wu_sem, wd_sem,
    f_zs, f_zr, f_ys, f_yr,
    r_ys, r_yr, r_zs, r_zr,
    a_zs, a_zr, a_ys, a_yr,
    pc_s, pc_r, px_s, px_r, dc_s, dc_r, dx_s, dx_r,
    q_s, q_r, qc_s, qc_r, nc_s, nc_r, nx_s, nx_r,
):
    n = Z * Y
    row, col = lax.axis_index("row"), lax.axis_index("col")
    z, y = row // Y, lax.rem(row, Y)
    x, core = col // CORES, lax.rem(col, CORES)
    X = Q // CORES
    tokens, width = normed.shape
    TB = tokens // Q

    def z_peer(d):
        return lax.rem(z + d, Z)

    def y_peer(d):
        return lax.rem(y + d, Y)

    def to_row(src, dst, send, recv, peer):
        return pltpu.make_async_remote_copy(
            src_ref=src, dst_ref=dst, send_sem=send, recv_sem=recv,
            device_id={"row": peer}, device_id_type=MESH,
        )

    def to_col(src, dst, send, recv, peer):
        return pltpu.make_async_remote_copy(
            src_ref=src, dst_ref=dst, send_sem=send, recv_sem=recv,
            device_id={"col": peer}, device_id_type=MESH,
        )

    def columns(c):
        return pl.ds(pl.multiple_of(c * C, C), C)

    def load_wo(f):
        return pltpu.make_async_copy(w_out.at[columns(f)], wo_buf.at[f], wo_sem.at[f])

    def load_gu(c):
        s = lax.rem(c, SLOTS)
        return (
            pltpu.make_async_copy(w_gate.at[:, columns(c)], wg_buf.at[s], wg_sem.at[s]),
            pltpu.make_async_copy(w_up.at[:, columns(c)], wu_buf.at[s], wu_sem.at[s]),
        )

    def load_wd(c):
        s = lax.rem(c, NF)
        return pltpu.make_async_copy(w_down.at[columns(c)], wo_buf.at[s], wd_sem.at[s])

    @pl.loop(0, NF)
    def _(f):
        load_wo(f).start()

    @pl.loop(0, SLOTS)
    def _(c):
        for copy in load_gu(c):
            copy.start()

    barrier = pltpu.get_barrier_semaphore()
    for d in range(1, n):
        pl.semaphore_signal(barrier, inc=1, device_id={"row": lax.rem(row + d, n)}, device_id_type=MESH)
    for d in range(1, Q):
        pl.semaphore_signal(barrier, inc=1, device_id={"col": lax.rem(col + d, Q)}, device_id_type=MESH)
    pl.semaphore_wait(barrier, n - 1 + Q - 1)

    def gather_z(buf, c, zs, zr):
        return [
            to_row(buf.at[c, y, z], buf.at[c, y, z], zs.at[c, d - 1], zr.at[c, d - 1], z_peer(d) * Y + y)
            for d in range(1, Z)
        ]

    def gather_y(buf, c, ys, yr):
        return [
            to_row(buf.at[c, y], buf.at[c, y], ys.at[c, d - 1], yr.at[c, d - 1], z * Y + y_peer(d))
            for d in range(1, Y)
        ]

    def reduce_cols(core_recv, x_recv, cs, cr, xs, xr):
        for r in range(n):
            at = ((r % Y) * Z + r // Y) * T
            q, off = (r * T) // TB, (r * T) % TB
            dsend[q % CORES, q // CORES, off : off + T] = acc[at : at + T].astype(BF16)
        order = [lax.rem(x + d, X) for d in (*range(1, X), 0)]
        core_copies = [
            to_col(dsend.at[1 - core, to], core_recv.at[i], cs.at[i], cr.at[i], x * CORES + 1 - core)
            for i, to in enumerate(order)
        ]
        for copy in core_copies:
            copy.start()
        x_copies = []
        for i, to in enumerate(order):
            core_copies[i].wait_recv()
            total = dsend[core, to].astype(F32) + core_recv[i].astype(F32)
            if i < X - 1:
                dsend[core, to] = total.astype(BF16)
                copy = to_col(dsend.at[core, to], x_recv.at[i], xs.at[i], xr.at[i], to * CORES + core)
                copy.start()
                x_copies.append(copy)
        for copy in core_copies:
            copy.wait_send()
        for i, copy in enumerate(x_copies):
            copy.wait()
            total = total + x_recv[i].astype(F32)
        return total

    for f in range(NF):
        feat[f, y, z] = attn[:, f * C : (f + 1) * C]
    acc[...] = jnp.zeros_like(acc)

    @pl.loop(0, NF)
    def _(f):
        for copy in gather_z(feat, f, f_zs, f_zr):
            copy.start()

    @pl.loop(0, NF + 1)
    def _(t):
        @pl.when(t < NF)
        def _():
            for copy in gather_z(feat, t, f_zs, f_zr):
                copy.wait_recv()
            for copy in gather_y(feat, t, f_ys, f_yr):
                copy.start()

        @pl.when(t >= 1)
        def _():
            f = t - 1
            for copy in gather_y(feat, f, f_ys, f_yr):
                copy.wait()
            for copy in gather_z(feat, f, f_zs, f_zr):
                copy.wait_send()
            load_wo(f).wait()
            acc[...] += jnp.dot(feat[f].reshape(tokens, C), wo_buf[f], preferred_element_type=F32)

    @pl.loop(0, min(NF, NC))
    def _(c):
        load_wd(c).start()

    stream_now = (resid[...].astype(F32) + reduce_cols(core_recv1, x_recv1, pc_s, pc_r, px_s, px_r)).astype(BF16)
    stream[...] = stream_now
    stream_f = stream_now.astype(F32)

    def block(q):
        return pl.ds(pl.multiple_of(q * TB, TB), TB)

    own = block(col)
    normed[own] = (stream_f * gain[...]).astype(BF16)

    def share(at, i):
        return to_col(normed.at[at], normed.at[at], nc_s.at[i], nc_r.at[i], x * CORES + 1 - core)

    x_copies = [
        to_col(normed.at[own], normed.at[own], nx_s.at[d - 1], nx_r.at[d - 1], lax.rem(x + d, X) * CORES + core)
        for d in range(1, X)
    ]
    shares = [share(own, 0)]
    for copy in x_copies + shares:
        copy.start()
    squares[own] = jnp.broadcast_to(jnp.sum(stream_f * stream_f, axis=1, keepdims=True), (TB, squares.shape[1]))
    sq_copies = [
        to_col(squares.at[own], squares.at[own], qc_s.at[d - 1], qc_r.at[d - 1], lax.rem(col + d, Q))
        for d in range(1, Q)
    ]
    for copy in sq_copies:
        copy.start()
    acc[...] = jnp.zeros_like(acc)
    for d in range(1, X):
        x_copies[d - 1].wait_recv()
        shares.append(share(block(lax.rem(x + X - d, X) * CORES + core), d))
        shares[d].start()
    for copy in sq_copies:
        copy.wait()

    def send_squares():
        copies = []
        for d in range(1, n):
            peer = lax.rem(row + d, n)
            src = squares.at[pl.ds(pl.multiple_of(peer * T, T), T)]
            copies.append(to_row(src, sq_recv.at[d - 1], q_s.at[d - 1], q_r.at[d - 1], peer))
        return copies

    for copy in send_squares():
        copy.start()
    for copy in x_copies:
        copy.wait_send()
    for copy in shares:
        copy.wait()

    def find_scale():
        total = squares[pl.ds(pl.multiple_of(row * T, T), T)]
        for d, copy in enumerate(send_squares()):
            copy.wait()
            total = total + sq_recv[d]
        scale[...] = lax.rsqrt(total / (width * n) + epsilon)

    def reduce_y(c):
        return [
            to_row(ysend.at[c, y_peer(d)], yrecv.at[c, d - 1], r_ys.at[c, d - 1], r_yr.at[c, d - 1], z * Y + y_peer(d))
            for d in range(1, Y)
        ]

    def reduce_z(c):
        return [
            to_row(ysend.at[c, y, z_peer(d)], zrecv.at[c, d - 1], r_zs.at[c, d - 1], r_zr.at[c, d - 1], z_peer(d) * Y + y)
            for d in range(1, Z)
        ]

    def multiply(c):
        s = lax.rem(c, SLOTS)
        gate_copy, up_copy = load_gu(c)
        for half, copy, buf in ((0, gate_copy, wg_buf), (1, up_copy, wu_buf)):
            copy.wait()
            part = jnp.dot(normed[...], buf[s], preferred_element_type=F32).astype(BF16)
            for r in range(n):
                ysend[c, r % Y, r // Y, :, half * C : (half + 1) * C] = part[r * T : (r + 1) * T]
        for copy in reduce_y(c):
            copy.start()

        @pl.when(c + SLOTS < NC)
        def _():
            for copy in load_gu(c + SLOTS):
                copy.start()

    def add_y(c):
        for copy in reduce_y(c):
            copy.wait_recv()
        total = ysend[c, y].astype(F32)
        for d in range(Y - 1):
            total = total + yrecv[c, d].astype(F32)
        ysend[c, y] = total.astype(BF16)
        for copy in reduce_z(c):
            copy.start()

    def activate(c):
        for copy in reduce_z(c):
            copy.wait_recv()
        total = ysend[c, y, z].astype(F32)
        for d in range(Z - 1):
            total = total + zrecv[c, d].astype(F32)
        by = scale[:, :1]
        gate, up = total[:, :C] * by, total[:, C:] * by
        act[c, y, z] = (gate / (1.0 + jnp.exp(-gate)) * up).astype(BF16)
        for copy in gather_z(act, c, a_zs, a_zr):
            copy.start()

    def pass_on(c):
        for copy in gather_z(act, c, a_zs, a_zr):
            copy.wait_recv()
        for copy in gather_y(act, c, a_ys, a_yr):
            copy.start()

    def project_down(c):
        for copy in gather_y(act, c, a_ys, a_yr):
            copy.wait()
        for copy in gather_z(act, c, a_zs, a_zr) + reduce_y(c) + reduce_z(c):
            copy.wait_send()
        load_wd(c).wait()
        acc[...] += jnp.dot(act[c].reshape(tokens, C), wo_buf[lax.rem(c, NF)], preferred_element_type=F32)

        @pl.when(c + NF < NC)
        def _():
            load_wd(c + NF).start()

    stages = ((0, multiply), (2, add_y), (3, activate), (4, pass_on), (6, project_down))

    @pl.loop(0, NC + 6)
    def _(t):
        @pl.when(t == 2)
        def _():
            find_scale()

        for lag, stage in stages:

            @pl.when((t >= lag) & (t < NC + lag))
            def _():
                stage(t - lag)

    out[...] = (stream[...].astype(F32) + reduce_cols(core_recv2, x_recv2, dc_s, dc_r, dx_s, dx_r)).astype(out.dtype)


def on_device(Z, Y, Q, attn_in, w_out, resid, norm_gain, w_gate, w_up, w_down):
    n = Z * Y
    T, features = attn_in.shape
    width, hidden = w_gate.shape
    tokens = T * n
    TB = tokens // Q
    X = Q // CORES
    C = chunk_of(hidden)
    NF, NC = features // C, hidden // C
    dma = pltpu.SemaphoreType.DMA
    vmem, hbm = pl.BlockSpec(memory_space=pltpu.VMEM), pl.BlockSpec(memory_space=pl.ANY)

    def pairs(count, peers):
        return [dma((count, peers)), dma((count, peers))]

    def both(peers):
        return [dma((peers,)), dma((peers,))]

    return pl.pallas_call(
        functools.partial(layer_kernel, Z, Y, Q, T, C, NF, NC),
        out_shape=jax.ShapeDtypeStruct((TB, width), BF16),
        in_specs=[vmem, hbm, vmem, vmem, hbm, hbm, hbm],
        out_specs=vmem,
        scratch_shapes=[
            pltpu.VMEM((NF, C, width), BF16),
            pltpu.VMEM((SLOTS, width, C), BF16),
            pltpu.VMEM((SLOTS, width, C), BF16),
            pltpu.VMEM((NF, Y, Z, T, C), BF16),
            pltpu.VMEM((NC, Y, Z, T, 2 * C), BF16),
            pltpu.VMEM((NC, Y - 1, Z, T, 2 * C), BF16),
            pltpu.VMEM((NC, Z - 1, T, 2 * C), BF16),
            pltpu.VMEM((NC, Y, Z, T, C), BF16),
            pltpu.VMEM((tokens, width), F32),
            pltpu.VMEM((tokens, width), BF16),
            pltpu.VMEM((TB, width), BF16),
            pltpu.VMEM((CORES, X, TB, width), BF16),
            pltpu.VMEM((X, TB, width), BF16),
            pltpu.VMEM((X - 1, TB, width), BF16),
            pltpu.VMEM((X, TB, width), BF16),
            pltpu.VMEM((X - 1, TB, width), BF16),
            pltpu.VMEM((tokens, 128), F32),
            pltpu.VMEM((n - 1, T, 128), F32),
            pltpu.VMEM((T, 128), F32),
            dma((NF,)), dma((SLOTS,)), dma((SLOTS,)), dma((NF,)),
            *pairs(NF, Z - 1), *pairs(NF, Y - 1),
            *pairs(NC, Y - 1), *pairs(NC, Z - 1),
            *pairs(NC, Z - 1), *pairs(NC, Y - 1),
            *both(X), *both(X - 1), *both(X), *both(X - 1),
            *both(n - 1), *both(Q - 1), *both(X), *both(X - 1),
        ],
        compiler_params=pltpu.CompilerParams(
            collective_id=0, has_side_effects=True, vmem_limit_bytes=60 * 2**20
        ),
    )(attn_in, w_out, resid, norm_gain.reshape(1, width), w_gate, w_up, w_down)


def solution(mesh):
    Z, Y = grid_of(mesh.shape["row"])
    placed = (
        P("row", "col"),
        P("col", "row"),
        P("col", "row"),
        P("row"),
        P("row", "col"),
        P("row", "col"),
        P("col", "row"),
    )
    return jax.shard_map(
        functools.partial(on_device, Z, Y, mesh.shape["col"]),
        mesh=mesh, in_specs=placed, out_specs=P("col", "row"), check_vma=False,
    )
```

```python
import functools

import jax
import jax.numpy as jnp
from jax import lax
from jax.experimental import pallas as pl
from jax.experimental.pallas import tpu as pltpu
from jax.sharding import PartitionSpec as P

MESH = pl.DeviceIdType.MESH
F32, BF16 = jnp.float32, jnp.bfloat16
epsilon = 1e-05
SLOTS = 6
CORES = 2


def chunk_of(hidden):
    return max(c for c in range(128, 257, 128) if hidden % c == 0)


def grid_of(rows):
    inner = 1
    while (2 * inner) ** 2 <= rows:
        inner *= 2
    return rows // inner, inner


def layer_kernel(
    Z, Y, Q, T, C, NF, NC,
    attn, w_out, resid, gain, w_gate, w_up, w_down,
    out,
    wo_buf, wg_buf, wu_buf,
    feat, ysend, yrecv, zrecv, act,
    acc, normed, stream, dsend, core_recv1, x_recv1, core_recv2, x_recv2, squares, sq_recv, scale,
    wo_sem, wg_sem, wu_sem, wd_sem,
    f_zs, f_zr, f_ys, f_yr,
    r_ys, r_yr, r_zs, r_zr,
    a_zs, a_zr, a_ys, a_yr,
    pc_s, pc_r, px_s, px_r, dc_s, dc_r, dx_s, dx_r,
    q_s, q_r, qc_s, qc_r, nc_s, nc_r, nx_s, nx_r,
):
    n = Z * Y
    row, col = lax.axis_index("row"), lax.axis_index("col")
    z, y = row // Y, lax.rem(row, Y)
    x, core = col // CORES, lax.rem(col, CORES)
    X = Q // CORES
    tokens, width = normed.shape
    TB = tokens // Q

    def z_peer(d):
        return lax.rem(z + d, Z)

    def y_peer(d):
        return lax.rem(y + d, Y)

    def to_row(src, dst, send, recv, peer):
        return pltpu.make_async_remote_copy(
            src_ref=src, dst_ref=dst, send_sem=send, recv_sem=recv,
            device_id={"row": peer}, device_id_type=MESH,
        )

    def to_col(src, dst, send, recv, peer):
        return pltpu.make_async_remote_copy(
            src_ref=src, dst_ref=dst, send_sem=send, recv_sem=recv,
            device_id={"col": peer}, device_id_type=MESH,
        )

    def columns(c):
        return pl.ds(pl.multiple_of(c * C, C), C)

    def load_wo(f):
        return pltpu.make_async_copy(w_out.at[columns(f)], wo_buf.at[f], wo_sem.at[f])

    def load_gu(c):
        s = lax.rem(c, SLOTS)
        return (
            pltpu.make_async_copy(w_gate.at[:, columns(c)], wg_buf.at[s], wg_sem.at[s]),
            pltpu.make_async_copy(w_up.at[:, columns(c)], wu_buf.at[s], wu_sem.at[s]),
        )

    def load_wd(c):
        s = lax.rem(c, NF)
        return pltpu.make_async_copy(w_down.at[columns(c)], wo_buf.at[s], wd_sem.at[s])

    @pl.loop(0, NF)
    def _(f):
        load_wo(f).start()

    @pl.loop(0, SLOTS)
    def _(c):
        for copy in load_gu(c):
            copy.start()

    barrier = pltpu.get_barrier_semaphore()
    for d in range(1, n):
        pl.semaphore_signal(barrier, inc=1, device_id={"row": lax.rem(row + d, n)}, device_id_type=MESH)
    for d in range(1, Q):
        pl.semaphore_signal(barrier, inc=1, device_id={"col": lax.rem(col + d, Q)}, device_id_type=MESH)
    pl.semaphore_wait(barrier, n - 1 + Q - 1)

    def gather_z(buf, c, zs, zr):
        return [
            to_row(buf.at[c, y, z], buf.at[c, y, z], zs.at[c, d - 1], zr.at[c, d - 1], z_peer(d) * Y + y)
            for d in range(1, Z)
        ]

    def gather_y(buf, c, ys, yr):
        return [
            to_row(buf.at[c, y], buf.at[c, y], ys.at[c, d - 1], yr.at[c, d - 1], z * Y + y_peer(d))
            for d in range(1, Y)
        ]

    def reduce_cols(core_recv, x_recv, cs, cr, xs, xr):
        for r in range(n):
            at = ((r % Y) * Z + r // Y) * T
            q, off = (r * T) // TB, (r * T) % TB
            dsend[q % CORES, q // CORES, off : off + T] = acc[at : at + T].astype(BF16)
        order = [lax.rem(x + d, X) for d in (*range(1, X), 0)]
        core_copies = [
            to_col(dsend.at[1 - core, to], core_recv.at[i], cs.at[i], cr.at[i], x * CORES + 1 - core)
            for i, to in enumerate(order)
        ]
        for copy in core_copies:
            copy.start()
        x_copies = []
        for i, to in enumerate(order):
            core_copies[i].wait_recv()
            total = dsend[core, to].astype(F32) + core_recv[i].astype(F32)
            if i < X - 1:
                dsend[core, to] = total.astype(BF16)
                copy = to_col(dsend.at[core, to], x_recv.at[i], xs.at[i], xr.at[i], to * CORES + core)
                copy.start()
                x_copies.append(copy)
        for copy in core_copies:
            copy.wait_send()
        for i, copy in enumerate(x_copies):
            copy.wait()
            total = total + x_recv[i].astype(F32)
        return total

    for f in range(NF):
        feat[f, y, z] = attn[:, f * C : (f + 1) * C]
    acc[...] = jnp.zeros_like(acc)

    @pl.loop(0, NF)
    def _(f):
        for copy in gather_z(feat, f, f_zs, f_zr):
            copy.start()

    @pl.loop(0, NF + 1)
    def _(t):
        @pl.when(t < NF)
        def _():
            for copy in gather_z(feat, t, f_zs, f_zr):
                copy.wait_recv()
            for copy in gather_y(feat, t, f_ys, f_yr):
                copy.start()

        @pl.when(t >= 1)
        def _():
            f = t - 1
            for copy in gather_y(feat, f, f_ys, f_yr):
                copy.wait()
            for copy in gather_z(feat, f, f_zs, f_zr):
                copy.wait_send()
            load_wo(f).wait()
            acc[...] += jnp.dot(feat[f].reshape(tokens, C), wo_buf[f], preferred_element_type=F32)

    @pl.loop(0, min(NF, NC))
    def _(c):
        load_wd(c).start()

    stream_now = (resid[...].astype(F32) + reduce_cols(core_recv1, x_recv1, pc_s, pc_r, px_s, px_r)).astype(BF16)
    stream[...] = stream_now
    stream_f = stream_now.astype(F32)

    def block(q):
        return pl.ds(pl.multiple_of(q * TB, TB), TB)

    own = block(col)
    normed[own] = (stream_f * gain[...]).astype(BF16)

    def share(at, i):
        return to_col(normed.at[at], normed.at[at], nc_s.at[i], nc_r.at[i], x * CORES + 1 - core)

    x_copies = [
        to_col(normed.at[own], normed.at[own], nx_s.at[d - 1], nx_r.at[d - 1], lax.rem(x + d, X) * CORES + core)
        for d in range(1, X)
    ]
    shares = [share(own, 0)]
    for copy in x_copies + shares:
        copy.start()
    squares[own] = jnp.broadcast_to(jnp.sum(stream_f * stream_f, axis=1, keepdims=True), (TB, squares.shape[1]))
    sq_copies = [
        to_col(squares.at[own], squares.at[own], qc_s.at[d - 1], qc_r.at[d - 1], lax.rem(col + d, Q))
        for d in range(1, Q)
    ]
    for copy in sq_copies:
        copy.start()
    acc[...] = jnp.zeros_like(acc)
    for d in range(1, X):
        x_copies[d - 1].wait_recv()
        shares.append(share(block(lax.rem(x + X - d, X) * CORES + core), d))
        shares[d].start()
    for copy in sq_copies:
        copy.wait()

    def send_squares():
        copies = []
        for d in range(1, n):
            peer = lax.rem(row + d, n)
            src = squares.at[pl.ds(pl.multiple_of(peer * T, T), T)]
            copies.append(to_row(src, sq_recv.at[d - 1], q_s.at[d - 1], q_r.at[d - 1], peer))
        return copies

    for copy in send_squares():
        copy.start()
    for copy in x_copies:
        copy.wait_send()
    for copy in shares:
        copy.wait()

    def find_scale():
        total = squares[pl.ds(pl.multiple_of(row * T, T), T)]
        for d, copy in enumerate(send_squares()):
            copy.wait()
            total = total + sq_recv[d]
        scale[...] = lax.rsqrt(total / (width * n) + epsilon)

    def reduce_y(c):
        return [
            to_row(ysend.at[c, y_peer(d)], yrecv.at[c, d - 1], r_ys.at[c, d - 1], r_yr.at[c, d - 1], z * Y + y_peer(d))
            for d in range(1, Y)
        ]

    def reduce_z(c):
        return [
            to_row(ysend.at[c, y, z_peer(d)], zrecv.at[c, d - 1], r_zs.at[c, d - 1], r_zr.at[c, d - 1], z_peer(d) * Y + y)
            for d in range(1, Z)
        ]

    def multiply(c):
        s = lax.rem(c, SLOTS)
        gate_copy, up_copy = load_gu(c)
        for half, copy, buf in ((0, gate_copy, wg_buf), (1, up_copy, wu_buf)):
            copy.wait()
            part = jnp.dot(normed[...], buf[s], preferred_element_type=F32).astype(BF16)
            for r in range(n):
                ysend[c, r % Y, r // Y, :, half * C : (half + 1) * C] = part[r * T : (r + 1) * T]
        for copy in reduce_y(c):
            copy.start()

        @pl.when(c + SLOTS < NC)
        def _():
            for copy in load_gu(c + SLOTS):
                copy.start()

    def add_y(c):
        for copy in reduce_y(c):
            copy.wait_recv()
        total = ysend[c, y].astype(F32)
        for d in range(Y - 1):
            total = total + yrecv[c, d].astype(F32)
        ysend[c, y] = total.astype(BF16)
        for copy in reduce_z(c):
            copy.start()

    def activate(c):
        for copy in reduce_z(c):
            copy.wait_recv()
        total = ysend[c, y, z].astype(F32)
        for d in range(Z - 1):
            total = total + zrecv[c, d].astype(F32)
        by = scale[:, :1]
        gate, up = total[:, :C] * by, total[:, C:] * by
        act[c, y, z] = (gate / (1.0 + jnp.exp(-gate)) * up).astype(BF16)
        for copy in gather_z(act, c, a_zs, a_zr):
            copy.start()

    def pass_on(c):
        for copy in gather_z(act, c, a_zs, a_zr):
            copy.wait_recv()
        for copy in gather_y(act, c, a_ys, a_yr):
            copy.start()

    def project_down(c):
        for copy in gather_y(act, c, a_ys, a_yr):
            copy.wait()
        for copy in gather_z(act, c, a_zs, a_zr) + reduce_y(c) + reduce_z(c):
            copy.wait_send()
        load_wd(c).wait()
        acc[...] += jnp.dot(act[c].reshape(tokens, C), wo_buf[lax.rem(c, NF)], preferred_element_type=F32)

        @pl.when(c + NF < NC)
        def _():
            load_wd(c + NF).start()

    stages = ((0, multiply), (3, add_y), (5, activate), (7, pass_on), (11, project_down))

    @pl.loop(0, NC + stages[-1][0])
    def _(t):
        @pl.when(t == 2)
        def _():
            find_scale()

        for lag, stage in stages:

            @pl.when((t >= lag) & (t < NC + lag))
            def _():
                stage(t - lag)

    out[...] = (stream[...].astype(F32) + reduce_cols(core_recv2, x_recv2, dc_s, dc_r, dx_s, dx_r)).astype(out.dtype)


def on_device(Z, Y, Q, attn_in, w_out, resid, norm_gain, w_gate, w_up, w_down):
    n = Z * Y
    T, features = attn_in.shape
    width, hidden = w_gate.shape
    tokens = T * n
    TB = tokens // Q
    X = Q // CORES
    C = chunk_of(hidden)
    NF, NC = features // C, hidden // C
    dma = pltpu.SemaphoreType.DMA
    vmem, hbm = pl.BlockSpec(memory_space=pltpu.VMEM), pl.BlockSpec(memory_space=pl.ANY)

    def pairs(count, peers):
        return [dma((count, peers)), dma((count, peers))]

    def both(peers):
        return [dma((peers,)), dma((peers,))]

    return pl.pallas_call(
        functools.partial(layer_kernel, Z, Y, Q, T, C, NF, NC),
        out_shape=jax.ShapeDtypeStruct((TB, width), BF16),
        in_specs=[vmem, hbm, vmem, vmem, hbm, hbm, hbm],
        out_specs=vmem,
        scratch_shapes=[
            pltpu.VMEM((NF, C, width), BF16),
            pltpu.VMEM((SLOTS, width, C), BF16),
            pltpu.VMEM((SLOTS, width, C), BF16),
            pltpu.VMEM((NF, Y, Z, T, C), BF16),
            pltpu.VMEM((NC, Y, Z, T, 2 * C), BF16),
            pltpu.VMEM((NC, Y - 1, Z, T, 2 * C), BF16),
            pltpu.VMEM((NC, Z - 1, T, 2 * C), BF16),
            pltpu.VMEM((NC, Y, Z, T, C), BF16),
            pltpu.VMEM((tokens, width), F32),
            pltpu.VMEM((tokens, width), BF16),
            pltpu.VMEM((TB, width), BF16),
            pltpu.VMEM((CORES, X, TB, width), BF16),
            pltpu.VMEM((X, TB, width), BF16),
            pltpu.VMEM((X - 1, TB, width), BF16),
            pltpu.VMEM((X, TB, width), BF16),
            pltpu.VMEM((X - 1, TB, width), BF16),
            pltpu.VMEM((tokens, 128), F32),
            pltpu.VMEM((n - 1, T, 128), F32),
            pltpu.VMEM((T, 128), F32),
            dma((NF,)), dma((SLOTS,)), dma((SLOTS,)), dma((NF,)),
            *pairs(NF, Z - 1), *pairs(NF, Y - 1),
            *pairs(NC, Y - 1), *pairs(NC, Z - 1),
            *pairs(NC, Z - 1), *pairs(NC, Y - 1),
            *both(X), *both(X - 1), *both(X), *both(X - 1),
            *both(n - 1), *both(Q - 1), *both(X), *both(X - 1),
        ],
        compiler_params=pltpu.CompilerParams(
            collective_id=0, has_side_effects=True, vmem_limit_bytes=60 * 2**20
        ),
    )(attn_in, w_out, resid, norm_gain.reshape(1, width), w_gate, w_up, w_down)


def solution(mesh):
    Z, Y = grid_of(mesh.shape["row"])
    placed = (
        P("row", "col"),
        P("col", "row"),
        P("col", "row"),
        P("row"),
        P("row", "col"),
        P("row", "col"),
        P("col", "row"),
    )
    return jax.shard_map(
        functools.partial(on_device, Z, Y, mesh.shape["col"]),
        mesh=mesh, in_specs=placed, out_specs=P("col", "row"), check_vma=False,
    )
```
